32 devices in a mesh: dp: 4 (over z), expert: 4 (over y, core), tensor: 2 (over x).
Axes of the slice: x: 2, y: 2, z: 4, core: 2. Of those that a mesh axis runs over, the one named last changes fastest.
Arguments:
- tokens: bfloat16 [144, 3072], P(('dp', 'expert'), 'tensor'), may hold values from -6 to 6
- cotangent: bfloat16 [144, 3072], P(('dp', 'expert'), 'tensor'), may hold values from -6 to 6
- routes: int32 [144, 4], P(('dp', 'expert')), may hold values from 0 to 15, all different within a row; in each aligned block of 9 rows (0 to 8, 9 to 17, ...) at most 3 rows name the same one
- gate_probs: float32 [144, 4], P(('dp', 'expert')), may hold values from 0.2 to 1
- gate_proj: bfloat16 [16, 3072, 6144], P('expert', 'tensor', 'dp'), may hold values from -0.109375 to 0.109375
- up_proj: bfloat16 [16, 3072, 6144], P('expert', 'tensor', 'dp'), may hold values from -0.109375 to 0.109375
- down_proj: bfloat16 [16, 6144, 3072], P('expert', 'dp', 'tensor'), may hold values from -0.078125 to 0.078125
Outputs:
- mixture_layer_output: bfloat16 [144, 3072], P(('dp', 'expert'), 'tensor')
- input_token_gradient: bfloat16 [144, 3072], P(('dp', 'expert'), 'tensor')
The draws below stay inside these ranges and needn't reach their ends.
Inputs may be any that keep to these rules, and one draw needn't show every extreme that they name: `routes`: each row names 4 different experts. Among the 9 rows of one device no expert is named more than 3 times, and in every draw some expert is named exactly 3 times by the rows of some device.
All inputs are finite; a program needn't handle non-finite values.
Results may differ from the reference program's by a relative error of at most 0.019.
Values may be sent and summed in bfloat16 or wider, within the bound.
A program may use at most 128 MiB of HBM per device.

```python
import math
import jax
import jax.numpy as jnp
import numpy as np
from jax import lax

D = 3072
EXPERT_HIDDEN = 6144
EXPERTS = 16
TOP = 4
TOK_DEV = 9
CAP = 3
TOKENS = 144
N_DP = 4
N_EXPERT = 4
N_TENSOR = 2


def steps_of(rng, extent, pieces, smallest, high):
    level, own = 1.0, jax.random.fold_in(rng, 6)
    for dim, blocks in pieces:
        steps = jnp.exp(jax.random.uniform(jax.random.fold_in(own, dim), (blocks,), jnp.float32, smallest / len(pieces), high / len(pieces)))
        level = level * jnp.repeat(steps, extent[dim] // blocks).reshape([-1 if axis == dim else 1 for axis in range(len(extent))])
    return level


def shared_out(key, own, number, rows, number_of, top, limit, skew):
    ranking = jax.random.permutation(key, number_of)
    heavy_load, common = load_shares(number_of, rows * top, limit, skew, True), load_shares(number_of, rows * top, limit, skew, False)
    places = jnp.arange(number_of)

    def named(lengths, rotation):
        used = int((lengths > 0).sum())
        fixed = max(1, used // 4)
        shifted = fixed + (places - fixed + rotation * (used - fixed)) % max(1, number_of - fixed)
        return jnp.zeros((number_of,), jnp.int32).at[ranking[jnp.where(places < fixed, places, shifted)]].set(jnp.asarray(lengths, jnp.int32))

    lengths = jnp.where(number % 4 == 0, named(heavy_load, number // 4), named(common, number - number // 4 - 1))
    mixed = jax.random.permutation(jax.random.fold_in(own, 3), number_of)
    giver, sink = mixed[0:number_of // 2 * 2:2], mixed[1:number_of // 2 * 2:2]
    room = jnp.minimum(lengths[giver] - 1, limit - lengths[sink]) // 2
    room = jnp.where((giver == ranking[0]) | (sink == ranking[0]) | (lengths[sink] == 0), 0, jnp.maximum(room, 0))
    shifted = jax.random.randint(jax.random.fold_in(own, 4), (number_of // 2,), 0, 1 << 20) % (room + 1)
    lengths = lengths.at[giver].add(-shifted).at[sink].add(shifted)
    items = jnp.searchsorted(jnp.cumsum(lengths), jnp.arange(rows * top), side="right").astype(jnp.int32)
    grid = items.reshape(top, rows).T
    grid = grid[jax.random.permutation(jax.random.fold_in(own, 1), rows)]
    rotation = jax.random.randint(jax.random.fold_in(own, 2), (rows, 1), 0, top)
    return jnp.take_along_axis(grid, (jnp.arange(top)[None, :] + rotation) % top, axis=1)


def load_shares(number_of, total, reach, slope, full):
    portions = [(1 << 20) // math.isqrt(standing ** slope) + 1 for standing in range(1, number_of + 1)]
    largest = reach if full else min(reach, max(-(-total // number_of), total * portions[0] // sum(portions)))
    least = 1 if total - largest >= number_of - 1 else 0
    counts, surplus = [largest] + [least] * (number_of - 1), total - largest - least * (number_of - 1)
    while surplus > 0:
        movable = [i for i in range(1, number_of) if counts[i] < largest] or [i for i in range(1, number_of) if counts[i] < reach]
        mass, budget = sum([portions[i] for i in movable]), surplus
        for i in movable:
            extra = min(reach - counts[i], max(1, budget * portions[i] // mass), surplus)
            counts[i] = counts[i] + extra
            surplus = surplus - extra
    return np.array(counts)


def bell_draw(rng, dims, scale, reach, split=(), held_as=jnp.bfloat16):
    values = scale * jax.random.normal(rng, dims, jnp.float32)
    if split:
        values = values * steps_of(rng, dims, split, -0.22, 0.18)
    return jnp.clip(values, -reach, reach).astype(held_as)


def setup_inputs(seed: int = 0) -> dict:
    streams_of = jax.random.split(jax.random.key(seed), 8)
    tokens = bell_draw(streams_of[0], (TOKENS, D), 1.0, 6.0, ((0, 16), (1, 2)))
    cotangent = bell_draw(streams_of[1], (TOKENS, D), 1.0, 6.0, ((0, 16), (1, 2)))
    routes_keys = jax.random.split(jax.random.fold_in(streams_of[2], 1), TOKENS // TOK_DEV)
    routes_turns = jax.random.permutation(jax.random.fold_in(streams_of[2], 3), TOKENS // TOK_DEV)
    routes = jax.vmap(lambda own, number: shared_out(jax.random.fold_in(streams_of[2], 2), own, number, TOK_DEV, EXPERTS, TOP, CAP, 2))(routes_keys, routes_turns).reshape((TOKENS, TOP))
    gate_probs = jnp.clip(0.2 + 0.8 * jax.random.uniform(streams_of[3], (TOKENS, TOP), jnp.float32) ** steps_of(streams_of[3], (TOKENS, TOP), ((0, 16),), -0.2, 0.2), 0.2, 1.0)
    gate_proj = bell_draw(streams_of[4], (EXPERTS, D, EXPERT_HIDDEN), D ** -0.5, 0.109375, ((0, 4), (1, 2), (2, 4)))
    up_proj = bell_draw(streams_of[5], (EXPERTS, D, EXPERT_HIDDEN), D ** -0.5, 0.109375, ((0, 4), (1, 2), (2, 4)))
    down_proj = bell_draw(streams_of[6], (EXPERTS, EXPERT_HIDDEN, D), EXPERT_HIDDEN ** -0.5, 0.078125, ((0, 4), (1, 4), (2, 2)))
    return {"tokens": tokens, "cotangent": cotangent, "routes": routes, "gate_probs": gate_probs, "gate_proj": gate_proj, "up_proj": up_proj, "down_proj": down_proj}


def slot_tables(routes, gate_probs, num_experts, capacity):
    tok_count = routes.shape[0]
    top_count = routes.shape[1]
    flat_ids = routes.reshape(-1)
    pair_count = flat_ids.shape[0]
    same_expert = (flat_ids[:, None] == flat_ids[None, :]).astype(jnp.int32)
    earlier = (lax.broadcasted_iota(jnp.int32, (pair_count, pair_count), 1) < lax.broadcasted_iota(jnp.int32, (pair_count, pair_count), 0)).astype(jnp.int32)
    slot_rank = jnp.sum(same_expert * earlier, axis=1)
    target = (flat_ids * capacity + slot_rank).reshape(tok_count, top_count)
    slot_ids = lax.broadcasted_iota(jnp.int32, (num_experts * capacity, tok_count, top_count), 0)
    matches = (slot_ids == target[None]).astype(jnp.float32)
    dispatch_tokens = jnp.sum(matches, axis=2)
    weighted_output_rows = jnp.sum(matches * gate_probs[None].astype(jnp.float32), axis=2)
    return dispatch_tokens, weighted_output_rows


def glu_terms(gate_activation_rows, up_activation_rows, backward_activation_rows):
    squashed = jax.nn.sigmoid(gate_activation_rows)
    swished = gate_activation_rows * squashed
    hidden = (swished * up_activation_rows).astype(jnp.bfloat16)
    grad_gate = (backward_activation_rows * up_activation_rows * squashed * (1.0 + gate_activation_rows * (1.0 - squashed))).astype(jnp.bfloat16)
    grad_up = (backward_activation_rows * swished).astype(jnp.bfloat16)
    return hidden, grad_gate, grad_up


def rounded_total_sum(partials):
    rounded = lax.optimization_barrier(partials.astype(jnp.bfloat16))
    return jnp.sum(rounded.astype(jnp.float32), axis=0)


def reference(tokens, cotangent, routes, gate_probs, gate_proj, up_proj, down_proj):
    blocks = N_DP * N_EXPERT
    quarter_slice = D // N_TENSOR
    share_width = EXPERT_HIDDEN // N_DP
    dispatch_tokens, weighted_output_rows = jax.vmap(lambda route_rows, prob_rows: slot_tables(route_rows, prob_rows, EXPERTS, CAP))(routes.reshape(blocks, TOK_DEV, TOP), gate_probs.reshape(blocks, TOK_DEV, TOP))
    token_block_rows = tokens.reshape(blocks, TOK_DEV, D).astype(jnp.float32)
    gradient_block_rows = cotangent.reshape(blocks, TOK_DEV, D).astype(jnp.float32)
    routed_token_rows = jnp.einsum("ypk,yka->ypa", dispatch_tokens, token_block_rows, precision=lax.Precision.HIGHEST).astype(jnp.bfloat16)
    routed_gradient_rows = jnp.einsum("ypk,yka->ypa", weighted_output_rows, gradient_block_rows, precision=lax.Precision.HIGHEST).astype(jnp.bfloat16)
    routed_token_rows = routed_token_rows.reshape(blocks, EXPERTS, CAP, D).transpose(1, 0, 2, 3)
    routed_gradient_rows = routed_gradient_rows.reshape(blocks, EXPERTS, CAP, D).transpose(1, 0, 2, 3)

    def one_expert(inputs):
        expert_rows, expert_grads, w_gate, w_up, w_down = inputs
        hidden_row_slice = expert_rows.reshape(-1, N_TENSOR, quarter_slice).astype(jnp.float32)
        hidden_gradient_slice = expert_grads.reshape(-1, N_TENSOR, quarter_slice).astype(jnp.float32)
        gate_weight_slice = w_gate.astype(jnp.float32)
        up_weight_slice = w_up.astype(jnp.float32)
        down_weight_slice = w_down.astype(jnp.float32)
        gate_activation_rows = rounded_total_sum(jnp.einsum("cia,iao->ico", hidden_row_slice, gate_weight_slice.reshape(N_TENSOR, quarter_slice, EXPERT_HIDDEN)))
        up_activation_rows = rounded_total_sum(jnp.einsum("cia,iao->ico", hidden_row_slice, up_weight_slice.reshape(N_TENSOR, quarter_slice, EXPERT_HIDDEN)))
        backward_activation_rows = rounded_total_sum(jnp.einsum("hyu,byu->yhb", hidden_gradient_slice, down_weight_slice.reshape(EXPERT_HIDDEN, N_TENSOR, quarter_slice)))
        hidden, grad_gate, grad_up = glu_terms(gate_activation_rows, up_activation_rows, backward_activation_rows)
        hidden_f = hidden.astype(jnp.float32).reshape(-1, N_DP, share_width)
        expert_out = rounded_total_sum(jnp.einsum("rpf,pfd->prd", hidden_f, down_weight_slice.reshape(N_DP, share_width, D))).astype(jnp.bfloat16)
        gate_part = jnp.einsum("rpf,dpf->prd", grad_gate.astype(jnp.float32).reshape(-1, N_DP, share_width), gate_weight_slice.reshape(D, N_DP, share_width))
        up_part = jnp.einsum("rpf,dpf->prd", grad_up.astype(jnp.float32).reshape(-1, N_DP, share_width), up_weight_slice.reshape(D, N_DP, share_width))
        expert_in_grad = rounded_total_sum(gate_part + up_part).astype(jnp.bfloat16)
        return expert_out, expert_in_grad

    expert_out, expert_in_grad = lax.map(one_expert, (routed_token_rows, routed_gradient_rows, gate_proj, up_proj, down_proj))
    output_slot_rows = expert_out.reshape(EXPERTS, blocks, CAP, D).transpose(1, 0, 2, 3).reshape(blocks, EXPERTS * CAP, D)
    gradient_slot_rows = expert_in_grad.reshape(EXPERTS, blocks, CAP, D).transpose(1, 0, 2, 3).reshape(blocks, EXPERTS * CAP, D)
    mixture_layer_output = jnp.einsum("woy,woh->wyh", weighted_output_rows, output_slot_rows.astype(jnp.float32), precision=lax.Precision.HIGHEST)
    input_token_gradient = jnp.einsum("woy,woh->wyh", dispatch_tokens, gradient_slot_rows.astype(jnp.float32), precision=lax.Precision.HIGHEST)
    return mixture_layer_output.reshape(TOKENS, D).astype(jnp.bfloat16), input_token_gradient.reshape(TOKENS, D).astype(jnp.bfloat16)
```

```python
import jax
import jax.numpy as jnp
from jax import lax
from jax.experimental import pallas as pl
from jax.experimental.pallas import tpu as pltpu
from jax.sharding import PartitionSpec as P

EXPERTS = 16
CAP = 3
VMEM_BYTES = 67000000


def slot_tables(routes, gate_probs, num_experts, capacity):
    tok_count = routes.shape[0]
    top_count = routes.shape[1]
    flat_ids = routes.reshape(-1)
    pair_count = flat_ids.shape[0]
    same_expert = (flat_ids[:, None] == flat_ids[None, :]).astype(jnp.int32)
    earlier = (
        lax.broadcasted_iota(jnp.int32, (pair_count, pair_count), 1)
        < lax.broadcasted_iota(jnp.int32, (pair_count, pair_count), 0)
    ).astype(jnp.int32)
    slot_rank = jnp.sum(same_expert * earlier, axis=1)
    target = (flat_ids * capacity + slot_rank).reshape(tok_count, top_count)
    slot_ids = lax.broadcasted_iota(jnp.int32, (num_experts * capacity, tok_count, top_count), 0)
    matches = (slot_ids == target[None]).astype(jnp.float32)
    dispatch_tokens = jnp.sum(matches, axis=2)
    weighted_output_rows = jnp.sum(matches * gate_probs[None], axis=2)
    return (dispatch_tokens, weighted_output_rows)


def glu_terms(gate_activation_rows, up_activation_rows, backward_activation_rows):
    squashed = jax.nn.sigmoid(gate_activation_rows)
    swished = gate_activation_rows * squashed
    hidden = (swished * up_activation_rows).astype(jnp.bfloat16)
    grad_gate = (
        backward_activation_rows
        * up_activation_rows
        * squashed
        * (1.0 + gate_activation_rows * (1.0 - squashed))
    ).astype(jnp.bfloat16)
    grad_up = (backward_activation_rows * swished).astype(jnp.bfloat16)
    return (hidden, grad_gate, grad_up)


def body(tokens, cotangent, routes, gate_probs, gate_proj, up_proj, down_proj):
    quarter_slice = tokens.shape[1]
    local_experts = gate_proj.shape[0]
    groups = lax.axis_size("expert")
    dispatch_tokens, weighted_output_rows = slot_tables(routes, gate_probs, EXPERTS, CAP)
    sent_tokens = jnp.dot(
        dispatch_tokens.astype(jnp.bfloat16), tokens, preferred_element_type=jnp.float32
    ).astype(jnp.bfloat16)
    sent_grads = jnp.dot(
        weighted_output_rows, cotangent.astype(jnp.float32), precision=lax.Precision.HIGHEST
    ).astype(jnp.bfloat16)
    sent_tokens = sent_tokens.reshape(EXPERTS, CAP, quarter_slice)
    sent_grads = sent_grads.reshape(EXPERTS, CAP, quarter_slice)
    got_tokens, got_grads = (
        lax.all_to_all(sent_tokens, "expert", split_axis=0, concat_axis=0, tiled=True),
        lax.all_to_all(sent_grads, "expert", split_axis=0, concat_axis=0, tiled=True),
    )
    got_tokens = got_tokens.reshape(groups, local_experts, CAP, quarter_slice)
    got_grads = got_grads.reshape(groups, local_experts, CAP, quarter_slice)
    row_tokens, row_grads = (
        lax.all_gather(got_tokens, "dp", axis=0, tiled=True),
        lax.all_gather(got_grads, "dp", axis=0, tiled=True),
    )
    gate_part = jnp.einsum(
        "becd,edf->becf", row_tokens, gate_proj, preferred_element_type=jnp.float32
    )
    up_part = jnp.einsum("becd,edf->becf", row_tokens, up_proj, preferred_element_type=jnp.float32)
    back_part = jnp.einsum(
        "becd,efd->becf", row_grads, down_proj, preferred_element_type=jnp.float32
    )
    gate_activation_rows, up_activation_rows, backward_activation_rows = (
        lax.psum(gate_part.astype(jnp.bfloat16), "tensor").astype(jnp.float32),
        lax.psum(up_part.astype(jnp.bfloat16), "tensor").astype(jnp.float32),
        lax.psum(back_part.astype(jnp.bfloat16), "tensor").astype(jnp.float32),
    )
    hidden, grad_gate, grad_up = glu_terms(
        gate_activation_rows, up_activation_rows, backward_activation_rows
    )
    out_rows = lax.psum_scatter(
        jnp.einsum("becf,efd->becd", hidden, down_proj, preferred_element_type=jnp.float32).astype(
            jnp.bfloat16
        ),
        "dp",
        scatter_dimension=0,
        tiled=True,
    ).astype(jnp.float32)
    from_gate = jnp.einsum(
        "becf,edf->becd", grad_gate, gate_proj, preferred_element_type=jnp.float32
    )
    from_up = jnp.einsum("becf,edf->becd", grad_up, up_proj, preferred_element_type=jnp.float32)
    in_rows = lax.psum_scatter(
        (from_gate + from_up).astype(jnp.bfloat16), "dp", scatter_dimension=0, tiled=True
    ).astype(jnp.float32)
    out_rows = out_rows.astype(jnp.bfloat16)
    in_rows = in_rows.astype(jnp.bfloat16)
    back_out, back_in = (
        lax.all_to_all(out_rows, "expert", split_axis=0, concat_axis=0, tiled=True),
        lax.all_to_all(in_rows, "expert", split_axis=0, concat_axis=0, tiled=True),
    )
    flat_out = back_out.reshape(EXPERTS * CAP, quarter_slice).astype(jnp.float32)
    flat_in = back_in.reshape(EXPERTS * CAP, quarter_slice).astype(jnp.float32)
    mixture_layer_output = jnp.dot(
        weighted_output_rows.T, flat_out, precision=lax.Precision.HIGHEST
    ).astype(jnp.bfloat16)
    input_token_gradient = jnp.dot(
        dispatch_tokens.T, flat_in, precision=lax.Precision.HIGHEST
    ).astype(jnp.bfloat16)
    return (mixture_layer_output, input_token_gradient)


PACK = 16
CHUNK = 256


def packed_rows(first, second):
    width = first.shape[1]
    split = PACK - first.shape[0]
    pieces = second[split:].reshape(-1, CHUNK)
    pieces = jnp.pad(pieces, ((0, PACK - pieces.shape[0]), (0, 0)))
    return jnp.concatenate([jnp.concatenate([first, second[:split]], axis=0), pieces], axis=1)


def unpacked_rows(packed, count):
    width = packed.shape[1] - CHUNK
    split = PACK - count
    pieces = (count - split) * width // CHUNK
    tail = packed[:pieces, width:].reshape(count - split, width)
    return packed[:count, :width], jnp.concatenate([packed[count:, :width], tail], axis=0)


def routing_table(routes, gate_probs, place, blocks, groups):
    count = routes.shape[0]
    local = EXPERTS // groups
    same = routes[None] == jnp.arange(EXPERTS)[:, None, None]
    hit = jnp.any(same, axis=2)
    prob = jnp.sum(jnp.where(same, gate_probs[None], 0.0), axis=2)
    before = jnp.arange(count)[None, :] < jnp.arange(count)[:, None]
    rank = jnp.sum(hit[:, None, :] & before[None], axis=2)
    mine = hit[:, None, :] & (rank[:, None, :] == jnp.arange(CAP)[None, :, None])
    rows = (place * PACK + 1 + jnp.arange(count)).astype(jnp.float32)
    token = jnp.sum(jnp.where(mine, rows[None, None], 0.0), axis=2)
    weight = jnp.sum(jnp.where(mine, prob[:, None, :], 0.0), axis=2)
    both = jnp.stack([token, weight]).reshape(2 * groups, local, 1, CAP)
    here = (jnp.arange(blocks) == place)[None, None, :, None]
    table = jnp.where(here, both, 0.0).reshape(2 * groups, local * blocks * CAP)
    return jnp.pad(table, ((0, 0), (0, 256 - table.shape[1])))


def nt_dot(a, b):
    return lax.dot_general(a, b, (((1,), (1,)), ((), ())), preferred_element_type=jnp.float32)


def nn_dot(a, b):
    return jnp.dot(a, b, preferred_element_type=jnp.float32)


def glu_kernel(
    x_ref, t_ref, wg_hbm, wu_hbm, wd_hbm, o_ref,
    w_v, gb, tab, xt, xg, pc, sbuf, rbuf, act, p_in, p_out, r1, s2, r2, s3, r3,
    w_sem, g_ss, g_rs, x_ss, x_rs, e_ss, e_rs,
):
    f32, bf16 = jnp.float32, jnp.bfloat16
    width = x_ref.shape[1] - CHUNK
    local, hidden_width = wg_hbm.shape[0], wg_hbm.shape[2]
    rows = sbuf.shape[2]
    slots = local * rows
    n_dp = lax.axis_size("dp")
    z, e, t = lax.axis_index("dp"), lax.axis_index("expert"), lax.axis_index("tensor")
    across = lax.rem(e + 2, 4)
    beside = e + 1 - 2 * lax.rem(e, 2)
    diagonal = lax.rem(beside + 2, 4)
    other = 1 - t
    span = n_dp * PACK

    hbm = (wg_hbm, wu_hbm, wd_hbm)

    def weight(m, j):
        return pltpu.make_async_copy(hbm[m].at[j], w_v.at[m, j], w_sem.at[m, j])

    def remote(src, dst, ss, rs, i, where):
        return pltpu.make_async_remote_copy(
            src_ref=src, dst_ref=dst, send_sem=ss.at[i], recv_sem=rs.at[i],
            device_id=where, device_id_type=pl.DeviceIdType.MESH,
        )

    def at_rows(k, n):
        return pl.ds(pl.multiple_of(k, PACK), n)

    barrier = pltpu.get_barrier_semaphore()
    partners = [{"dp": lax.rem(z + d, n_dp)} for d in range(1, n_dp)]
    partners += [{"expert": across}, {"expert": beside}, {"tensor": other}]
    for p in partners:
        pl.semaphore_signal(barrier, inc=1, device_id=p, device_id_type=pl.DeviceIdType.MESH)
    for j in range(local):
        for m in range(3):
            weight(m, j).start()
    place = e * n_dp + z
    own = at_rows(place * PACK, PACK)
    gb[own, :] = x_ref[...]
    tab[pl.ds(place, 1)] = t_ref[...][None]
    p_in[slots:, :] = jnp.zeros((p_in.shape[0] - slots, width), bf16)
    p_out[slots:, :] = jnp.zeros((p_out.shape[0] - slots, width), bf16)
    pl.semaphore_wait(barrier, len(partners))

    first = []
    for d in range(1, n_dp):
        to = {"dp": lax.rem(z + d, n_dp)}
        first.append(remote(gb.at[own], gb.at[own], g_ss, g_rs, 2 * d - 2, to))
        first.append(
            remote(tab.at[pl.ds(place, 1)], tab.at[pl.ds(place, 1)], g_ss, g_rs, 2 * d - 1, to)
        )
    for c in first:
        c.start()
    for c in first:
        c.wait_recv()

    def send_group(k, group, to):
        a = at_rows(group * span, span)
        b = pl.ds(group * n_dp, n_dp)
        pair = [
            remote(gb.at[a], gb.at[a], g_ss, g_rs, k, to),
            remote(tab.at[b], tab.at[b], g_ss, g_rs, k + 1, to),
        ]
        for c in pair:
            c.start()
        return pair

    second = send_group(6, e, {"expert": across})
    third = send_group(8, e, {"expert": beside})
    for c in second:
        c.wait_recv()
    fourth = send_group(10, across, {"expert": beside})
    for c in third + fourth:
        c.wait_recv()

    row_of = jnp.sum(tab[:, pl.ds(e, 1), :], axis=0)
    prob_of = jnp.sum(tab[:, pl.ds(e + 4, 1), :], axis=0)

    def keys(v):
        k = v - 1.0
        base = jnp.floor(k * (1.0 / PACK)) * PACK
        r = k - base
        tokens_count = 9.0
        split = PACK - tokens_count
        second_key = jnp.where(r < split, k + tokens_count, -1.0)
        tail_key = jnp.where(
            (r >= split) & (r < tokens_count), base + (r - split) * (width // CHUNK), -1000.0
        )
        return k.astype(jnp.int32), second_key.astype(jnp.int32), tail_key.astype(jnp.int32)

    def one_hot(hit):
        return jnp.where(hit, 1.0, 0.0).astype(bf16)

    column = jnp.transpose(jnp.broadcast_to(row_of, (128, row_of.shape[1])))[:slots]
    pc[...] = jnp.transpose(jnp.broadcast_to(prob_of, (128, prob_of.shape[1])))[:slots]
    wide = jnp.concatenate([column, column], axis=1)
    k1, k2, k3 = keys(wide)
    lane = lax.broadcasted_iota(jnp.int32, (slots, 256), 1)
    pick_first, pick_second = one_hot(k1 == lane), one_hot(k2 == lane)
    scale = pc[:, 0:1]
    for q in range(width // CHUNK):
        cols = pl.ds(q * CHUNK, CHUNK)
        xt[:, cols] = nn_dot(pick_first, gb[:, cols]).astype(bf16)
        g = nn_dot(pick_second, gb[:, cols])
        g += nn_dot(one_hot(k3 + q == lane), gb[:, width:])
        xg[:, cols] = (scale * g).astype(bf16)

    def act_copy(j, m):
        return pltpu.make_async_remote_copy(
            src_ref=sbuf.at[j, m], dst_ref=rbuf.at[j, m],
            send_sem=x_ss.at[j, m], recv_sem=x_rs.at[j, m],
            device_id={"tensor": other}, device_id_type=pl.DeviceIdType.MESH,
        )

    def project(j, carry):
        mine = at_rows(j * rows, rows)
        for m in range(3):
            weight(m, j).wait()

            def tile(n, c):
                cols = pl.ds(pl.multiple_of(n * CHUNK, CHUNK), CHUNK)
                if m < 2:
                    part = nn_dot(xt[mine, :], w_v[m, j, :, cols])
                else:
                    part = nt_dot(xg[mine, :], w_v[m, j, cols, :])
                sbuf[j, m, :, cols] = part.astype(bf16)
                return c

            lax.fori_loop(0, hidden_width // CHUNK, tile, 0)
            act_copy(j, m).start()
        return carry

    lax.fori_loop(0, local, project, 0)

    def finish(j, carry):
        mine = at_rows(j * rows, rows)
        for m in range(3):
            act_copy(j, m).wait_recv()

        def terms(n, c):
            cols = pl.ds(pl.multiple_of(n * CHUNK, CHUNK), CHUNK)
            total = [
                sbuf[j, m, :, cols].astype(f32) + rbuf[j, m, :, cols].astype(f32) for m in range(3)
            ]
            for m, v in enumerate(glu_terms(*total)):
                act[m, :, cols] = v
            return c

        lax.fori_loop(0, hidden_width // CHUNK, terms, 0)
        by = pc[mine, 0:1]

        def tile(n, c):
            cols = pl.ds(pl.multiple_of(n * CHUNK, CHUNK), CHUNK)
            out = nn_dot(act[0], w_v[2, j, :, cols])
            p_out[mine, cols] = (by * out).astype(bf16)
            back = nt_dot(act[1], w_v[0, j, cols, :]) + nt_dot(act[2], w_v[1, j, cols, :])
            p_in[mine, cols] = back.astype(bf16)
            return c

        lax.fori_loop(0, width // CHUNK, tile, 0)
        return carry

    lax.fori_loop(0, local, finish, 0)

    for c in first + second + third + fourth:
        c.wait_send()
    acc = gb
    n1, n2, n3 = keys(row_of)
    down = lax.broadcasted_iota(jnp.int32, (gb.shape[0], row_of.shape[1]), 0)
    put_first, put_second = one_hot(n1 == down), one_hot(n2 == down)
    tail = jnp.zeros((gb.shape[0], CHUNK), f32)
    for q in range(width // CHUNK):
        cols = pl.ds(q * CHUNK, CHUNK)
        v = nn_dot(put_first, p_in[:, cols]) + nn_dot(put_second, p_out[:, cols])
        acc[:, cols] = v.astype(bf16)
        tail += nn_dot(one_hot(n3 + q == down), p_out[:, cols])
    acc[:, width:] = tail.astype(bf16)

    a1 = remote(acc.at[at_rows(diagonal * span, span)], r1.at[1], e_ss, e_rs, 0, {"expert": beside})
    a0 = remote(acc.at[at_rows(beside * span, span)], r1.at[0], e_ss, e_rs, 1, {"expert": beside})
    a1.start()
    a0.start()
    a1.wait_recv()
    s2[...] = (acc[at_rows(across * span, span), :].astype(f32) + r1[1].astype(f32)).astype(bf16)
    b = remote(s2, r2, e_ss, e_rs, 2, {"expert": across})
    b.start()
    a0.wait_recv()
    held = acc[at_rows(e * span, span), :].astype(f32) + r1[0].astype(f32)
    b.wait_recv()
    s3[...] = (held + r2[...].astype(f32)).astype(bf16)
    last = []
    for d in range(1, n_dp):
        to = lax.rem(z + d, n_dp)
        c = remote(
            s3.at[at_rows(to * PACK, PACK)], r3.at[d - 1], e_ss, e_rs, 2 + d, {"dp": to}
        )
        c.start()
        last.append(c)
    final = s3[at_rows(z * PACK, PACK), :].astype(f32)
    for d, c in enumerate(last):
        c.wait_recv()
        final += r3[d].astype(f32)
    o_ref[...] = final.astype(bf16)

    for c in [a1, a0, b] + last:
        c.wait_send()

    def sent(j, carry):
        for m in range(3):
            act_copy(j, m).wait_send()
        return carry

    lax.fori_loop(0, local, sent, 0)


def kernel_body(tokens, cotangent, routes, gate_probs, gate_proj, up_proj, down_proj):
    groups, n_dp = lax.axis_size("expert"), lax.axis_size("dp")
    blocks = groups * n_dp
    place = lax.axis_index("expert") * n_dp + lax.axis_index("dp")
    count, width = tokens.shape
    local, _, hidden_width = gate_proj.shape
    rows = blocks * CAP
    packed = packed_rows(tokens, cotangent)
    table = routing_table(routes, gate_probs, place, blocks, groups)
    bf16, dma = jnp.bfloat16, pltpu.SemaphoreType.DMA
    full, span = width + CHUNK, n_dp * PACK
    out = pl.pallas_call(
        glu_kernel,
        out_shape=jax.ShapeDtypeStruct((PACK, full), bf16),
        in_specs=[pl.BlockSpec(memory_space=pltpu.VMEM)] * 2
        + [pl.BlockSpec(memory_space=pl.ANY)] * 3,
        out_specs=pl.BlockSpec(memory_space=pltpu.VMEM),
        scratch_shapes=[
            pltpu.VMEM((3, local, width, hidden_width), bf16),
            pltpu.VMEM((blocks * PACK, full), bf16),
            pltpu.VMEM((blocks, 8, 256), jnp.float32),
            pltpu.VMEM((local * rows, width), bf16),
            pltpu.VMEM((local * rows, width), bf16),
            pltpu.VMEM((local * rows, 128), jnp.float32),
            pltpu.VMEM((local, 3, rows, hidden_width), bf16),
            pltpu.VMEM((local, 3, rows, hidden_width), bf16),
            pltpu.VMEM((3, rows, hidden_width), bf16),
            pltpu.VMEM((256, width), bf16),
            pltpu.VMEM((256, width), bf16),
            pltpu.VMEM((2, span, full), bf16),
            pltpu.VMEM((span, full), bf16),
            pltpu.VMEM((span, full), bf16),
            pltpu.VMEM((span, full), bf16),
            pltpu.VMEM((n_dp - 1, PACK, full), bf16),
            dma((3, local)),
            dma((12,)),
            dma((12,)),
            dma((local, 3)),
            dma((local, 3)),
            dma((6,)),
            dma((6,)),
        ],
        compiler_params=pltpu.CompilerParams(
            collective_id=0, has_side_effects=True, vmem_limit_bytes=VMEM_BYTES
        ),
    )(packed, table, gate_proj, up_proj, down_proj)
    in_grad, layer_out = unpacked_rows(out, count)
    return layer_out, in_grad


def solution(mesh):
    in_specs = (
        P(("dp", "expert"), "tensor"),
        P(("dp", "expert"), "tensor"),
        P(("dp", "expert"), None),
        P(("dp", "expert"), None),
        P("expert", "tensor", "dp"),
        P("expert", "tensor", "dp"),
        P("expert", "dp", "tensor"),
    )
    out_specs = (P(("dp", "expert"), "tensor"), P(("dp", "expert"), "tensor"))
    small = (mesh.shape["dp"], mesh.shape["expert"], mesh.shape["tensor"]) == (4, 4, 2)
    return jax.shard_map(
        kernel_body if small else body,
        mesh=mesh, in_specs=in_specs, out_specs=out_specs, check_vma=False,
    )
```

```python
import jax
import jax.numpy as jnp
from jax import lax
from jax.experimental import pallas as pl
from jax.experimental.pallas import tpu as pltpu
from jax.sharding import PartitionSpec as P

EXPERTS = 16
CAP = 3
VMEM_BYTES = 67000000


def slot_tables(routes, gate_probs, num_experts, capacity):
    tok_count = routes.shape[0]
    top_count = routes.shape[1]
    flat_ids = routes.reshape(-1)
    pair_count = flat_ids.shape[0]
    same_expert = (flat_ids[:, None] == flat_ids[None, :]).astype(jnp.int32)
    earlier = (
        lax.broadcasted_iota(jnp.int32, (pair_count, pair_count), 1)
        < lax.broadcasted_iota(jnp.int32, (pair_count, pair_count), 0)
    ).astype(jnp.int32)
    slot_rank = jnp.sum(same_expert * earlier, axis=1)
    target = (flat_ids * capacity + slot_rank).reshape(tok_count, top_count)
    slot_ids = lax.broadcasted_iota(jnp.int32, (num_experts * capacity, tok_count, top_count), 0)
    matches = (slot_ids == target[None]).astype(jnp.float32)
    dispatch_tokens = jnp.sum(matches, axis=2)
    weighted_output_rows = jnp.sum(matches * gate_probs[None], axis=2)
    return (dispatch_tokens, weighted_output_rows)


def glu_terms(gate_activation_rows, up_activation_rows, backward_activation_rows):
    squashed = jax.nn.sigmoid(gate_activation_rows)
    swished = gate_activation_rows * squashed
    hidden = (swished * up_activation_rows).astype(jnp.bfloat16)
    grad_gate = (
        backward_activation_rows
        * up_activation_rows
        * squashed
        * (1.0 + gate_activation_rows * (1.0 - squashed))
    ).astype(jnp.bfloat16)
    grad_up = (backward_activation_rows * swished).astype(jnp.bfloat16)
    return (hidden, grad_gate, grad_up)


def body(tokens, cotangent, routes, gate_probs, gate_proj, up_proj, down_proj):
    quarter_slice = tokens.shape[1]
    local_experts = gate_proj.shape[0]
    groups = lax.axis_size("expert")
    dispatch_tokens, weighted_output_rows = slot_tables(routes, gate_probs, EXPERTS, CAP)
    sent_tokens = jnp.dot(
        dispatch_tokens.astype(jnp.bfloat16), tokens, preferred_element_type=jnp.float32
    ).astype(jnp.bfloat16)
    sent_grads = jnp.dot(
        weighted_output_rows, cotangent.astype(jnp.float32), precision=lax.Precision.HIGHEST
    ).astype(jnp.bfloat16)
    sent_tokens = sent_tokens.reshape(EXPERTS, CAP, quarter_slice)
    sent_grads = sent_grads.reshape(EXPERTS, CAP, quarter_slice)
    got_tokens, got_grads = (
        lax.all_to_all(sent_tokens, "expert", split_axis=0, concat_axis=0, tiled=True),
        lax.all_to_all(sent_grads, "expert", split_axis=0, concat_axis=0, tiled=True),
    )
    got_tokens = got_tokens.reshape(groups, local_experts, CAP, quarter_slice)
    got_grads = got_grads.reshape(groups, local_experts, CAP, quarter_slice)
    row_tokens, row_grads = (
        lax.all_gather(got_tokens, "dp", axis=0, tiled=True),
        lax.all_gather(got_grads, "dp", axis=0, tiled=True),
    )
    gate_part = jnp.einsum(
        "becd,edf->becf", row_tokens, gate_proj, preferred_element_type=jnp.float32
    )
    up_part = jnp.einsum("becd,edf->becf", row_tokens, up_proj, preferred_element_type=jnp.float32)
    back_part = jnp.einsum(
        "becd,efd->becf", row_grads, down_proj, preferred_element_type=jnp.float32
    )
    gate_activation_rows, up_activation_rows, backward_activation_rows = (
        lax.psum(gate_part.astype(jnp.bfloat16), "tensor").astype(jnp.float32),
        lax.psum(up_part.astype(jnp.bfloat16), "tensor").astype(jnp.float32),
        lax.psum(back_part.astype(jnp.bfloat16), "tensor").astype(jnp.float32),
    )
    hidden, grad_gate, grad_up = glu_terms(
        gate_activation_rows, up_activation_rows, backward_activation_rows
    )
    out_rows = lax.psum_scatter(
        jnp.einsum("becf,efd->becd", hidden, down_proj, preferred_element_type=jnp.float32).astype(
            jnp.bfloat16
        ),
        "dp",
        scatter_dimension=0,
        tiled=True,
    ).astype(jnp.float32)
    from_gate = jnp.einsum(
        "becf,edf->becd", grad_gate, gate_proj, preferred_element_type=jnp.float32
    )
    from_up = jnp.einsum("becf,edf->becd", grad_up, up_proj, preferred_element_type=jnp.float32)
    in_rows = lax.psum_scatter(
        (from_gate + from_up).astype(jnp.bfloat16), "dp", scatter_dimension=0, tiled=True
    ).astype(jnp.float32)
    out_rows = out_rows.astype(jnp.bfloat16)
    in_rows = in_rows.astype(jnp.bfloat16)
    back_out, back_in = (
        lax.all_to_all(out_rows, "expert", split_axis=0, concat_axis=0, tiled=True),
        lax.all_to_all(in_rows, "expert", split_axis=0, concat_axis=0, tiled=True),
    )
    flat_out = back_out.reshape(EXPERTS * CAP, quarter_slice).astype(jnp.float32)
    flat_in = back_in.reshape(EXPERTS * CAP, quarter_slice).astype(jnp.float32)
    mixture_layer_output = jnp.dot(
        weighted_output_rows.T, flat_out, precision=lax.Precision.HIGHEST
    ).astype(jnp.bfloat16)
    input_token_gradient = jnp.dot(
        dispatch_tokens.T, flat_in, precision=lax.Precision.HIGHEST
    ).astype(jnp.bfloat16)
    return (mixture_layer_output, input_token_gradient)


PACK = 16
CHUNK = 256
FIRST = 1024


def nt_dot(a, b):
    return lax.dot_general(a, b, (((1,), (1,)), ((), ())), preferred_element_type=jnp.float32)


def nn_dot(a, b):
    return jnp.dot(a, b, preferred_element_type=jnp.float32)


def glu_kernel(
    tok_ref, cot_ref, route_ref, prob_ref, wg_hbm, wu_hbm, wd_hbm, out_ref, grad_ref,
    w_v, gb, tab, xt, xg, pc, sbuf, rbuf, act, p_in, p_out, r1, s2, r2, s3, r3, r3b, s4, s5, r5,
    w_sem, g_ss, g_rs, x_ss, x_rs, e_ss, e_rs,
):
    f32, bf16 = jnp.float32, jnp.bfloat16
    count, width = tok_ref.shape
    split = PACK - count
    pieces = width // CHUNK
    local, hidden_width = wg_hbm.shape[0], wg_hbm.shape[2]
    rows = sbuf.shape[2]
    slots = local * rows
    n_dp = lax.axis_size("dp")
    z, e, t = lax.axis_index("dp"), lax.axis_index("expert"), lax.axis_index("tensor")
    across = lax.rem(e + 2, 4)
    beside = e + 1 - 2 * lax.rem(e, 2)
    diagonal = lax.rem(beside + 2, 4)
    other = 1 - t
    span = n_dp * PACK

    hbm = (wg_hbm, wu_hbm, wd_hbm)

    def weight(m, j):
        return pltpu.make_async_copy(hbm[m].at[j], w_v.at[m, j], w_sem.at[m, j])

    def remote(src, dst, ss, rs, i, where):
        return pltpu.make_async_remote_copy(
            src_ref=src, dst_ref=dst, send_sem=ss.at[i], recv_sem=rs.at[i],
            device_id=where, device_id_type=pl.DeviceIdType.MESH,
        )

    def at_rows(k, n):
        return pl.ds(pl.multiple_of(k, PACK), n)

    barrier = pltpu.get_barrier_semaphore()
    partners = [{"dp": lax.rem(z + d, n_dp)} for d in range(1, n_dp)]
    partners += [{"expert": across}, {"expert": beside}, {"tensor": other}]
    for p in partners:
        pl.semaphore_signal(barrier, inc=1, device_id=p, device_id_type=pl.DeviceIdType.MESH)
    for j in range(local):
        for m in range(3):
            weight(m, j).start()
    place = e * n_dp + z
    own = at_rows(place * PACK, PACK)
    tokens, cotangent = tok_ref[...].astype(f32), cot_ref[...].astype(f32)
    gb[own, :width] = jnp.concatenate([tokens, cotangent[:split]], axis=0).astype(bf16)
    tail = [
        cotangent[r : r + 1, q * CHUNK : (q + 1) * CHUNK]
        for r in range(split, count)
        for q in range(pieces)
    ]
    tail.append(jnp.zeros((PACK - len(tail), CHUNK), f32))
    gb[own, width:] = jnp.concatenate(tail, axis=0).astype(bf16)
    lane = lax.broadcasted_iota(jnp.int32, (8, 256), 1).astype(f32)
    group = lax.broadcasted_iota(jnp.int32, (8, 256), 0)
    expert = jnp.floor((lane + 0.5) / rows)
    within = lane - expert * rows
    block = jnp.floor((within + 0.5) / CAP)
    nth = (within - block * CAP).astype(jnp.int32)
    here = (block.astype(jnp.int32) == place) & (expert < local)
    expert = expert.astype(jnp.int32) + lax.rem(group, 4) * local
    seen = jnp.zeros((8, 256), jnp.int32)
    token = jnp.zeros((8, 256), f32)
    chance = jnp.zeros((8, 256), f32)
    for r in range(count):
        hits = jnp.zeros((8, 256), jnp.int32)
        for k in range(route_ref.shape[1]):
            hit = expert == route_ref[r, k]
            hits += hit.astype(jnp.int32)
            chance = jnp.where(hit & here & (seen == nth), prob_ref[r, k], chance)
        key = (place * PACK + 1 + r).astype(f32)
        token = jnp.where((hits > 0) & here & (seen == nth), key, token)
        seen += hits
    tab[pl.ds(place, 1)] = jnp.where(group < 4, token, chance)[None]
    p_in[slots:, :] = jnp.zeros((p_in.shape[0] - slots, width), bf16)
    p_out[slots:, :] = jnp.zeros((p_out.shape[0] - slots, width), bf16)
    pl.semaphore_wait(barrier, len(partners))

    wide_cols = (pl.ds(0, FIRST), pl.ds(FIRST, width + CHUNK - FIRST))

    def send(sent, src, to):
        i = len(started)
        c = remote(src, src, g_ss, g_rs, i, to)
        c.start()
        started.append(c)
        sent.append(c)

    def arrived(sent):
        for c in sent:
            c.wait_recv()

    def group_at(g, h):
        return gb.at[at_rows(g * span, span), wide_cols[h]]

    def table_at(g):
        return tab.at[pl.ds(g * n_dp, n_dp)]

    started, along, over = [], [], []
    one = tab.at[pl.ds(place, 1)]
    send(over, gb.at[own, wide_cols[1]], {"expert": across})
    for d in range(1, n_dp):
        to = {"dp": lax.rem(z + d, n_dp)}
        send(along, gb.at[own, wide_cols[0]], to)
        send(along, one, to)
    arrived(over)
    along_two, over_two, side = [], [], []
    facing = at_rows((across * n_dp + z) * PACK, PACK)
    for d in range(1, n_dp):
        to = {"dp": lax.rem(z + d, n_dp)}
        send(along_two, gb.at[own, wide_cols[1]], to)
        send(along_two, gb.at[facing, wide_cols[1]], to)
    arrived(along)
    send(over_two, group_at(e, 0), {"expert": across})
    send(over_two, table_at(e), {"expert": across})
    send(side, group_at(e, 0), {"expert": beside})
    send(side, table_at(e), {"expert": beside})
    arrived(along_two)
    send(side, group_at(e, 1), {"expert": beside})
    send(side, group_at(across, 1), {"expert": beside})
    arrived(over_two)
    send(side, group_at(across, 0), {"expert": beside})
    send(side, table_at(across), {"expert": beside})
    arrived(side)

    row_of = jnp.sum(tab[:, pl.ds(e, 1), :], axis=0)
    prob_of = jnp.sum(tab[:, pl.ds(e + 4, 1), :], axis=0)

    def keys(v):
        k = v - 1.0
        base = jnp.floor(k * (1.0 / PACK)) * PACK
        r = k - base
        second_key = jnp.where(r < split, k + count, -1.0)
        tail_key = jnp.where((r >= split) & (r < count), base + (r - split) * pieces, -1000.0)
        return k.astype(jnp.int32), second_key.astype(jnp.int32), tail_key.astype(jnp.int32)

    def one_hot(hit):
        return jnp.where(hit, 1.0, 0.0).astype(bf16)

    column = jnp.transpose(jnp.broadcast_to(row_of, (128, row_of.shape[1])))[:slots]
    pc[...] = jnp.transpose(jnp.broadcast_to(prob_of, (128, prob_of.shape[1])))[:slots]
    wide = jnp.concatenate([column, column], axis=1)
    k1, k2, k3 = keys(wide)
    lane = lax.broadcasted_iota(jnp.int32, (slots, 256), 1)
    pick_first, pick_second = one_hot(k1 == lane), one_hot(k2 == lane)
    scale = pc[:, 0:1]
    for q in range(width // CHUNK):
        cols = pl.ds(q * CHUNK, CHUNK)
        xt[:, cols] = nn_dot(pick_first, gb[:, cols]).astype(bf16)
        g = nn_dot(pick_second, gb[:, cols])
        g += nn_dot(one_hot(k3 + q == lane), gb[:, width:])
        xg[:, cols] = (scale * g).astype(bf16)

    def act_copy(j, m):
        return pltpu.make_async_remote_copy(
            src_ref=sbuf.at[j, m], dst_ref=rbuf.at[j, m],
            send_sem=x_ss.at[j, m], recv_sem=x_rs.at[j, m],
            device_id={"tensor": other}, device_id_type=pl.DeviceIdType.MESH,
        )

    def project(j, carry):
        mine = at_rows(j * rows, rows)
        for m in range(3):
            weight(m, j).wait()

            def tile(n, c):
                cols = pl.ds(pl.multiple_of(n * CHUNK, CHUNK), CHUNK)
                if m < 2:
                    part = nn_dot(xt[mine, :], w_v[m, j, :, cols])
                else:
                    part = nt_dot(xg[mine, :], w_v[m, j, cols, :])
                sbuf[j, m, :, cols] = part.astype(bf16)
                return c

            lax.fori_loop(0, hidden_width // CHUNK, tile, 0)
            act_copy(j, m).start()
        return carry

    lax.fori_loop(0, local, project, 0)

    def finish(j, carry):
        mine = at_rows(j * rows, rows)
        for m in range(3):
            act_copy(j, m).wait_recv()

        def terms(n, c):
            cols = pl.ds(pl.multiple_of(n * CHUNK, CHUNK), CHUNK)
            total = [
                sbuf[j, m, :, cols].astype(f32) + rbuf[j, m, :, cols].astype(f32) for m in range(3)
            ]
            for m, v in enumerate(glu_terms(*total)):
                act[m, :, cols] = v
            return c

        lax.fori_loop(0, hidden_width // CHUNK, terms, 0)
        by = pc[mine, 0:1]

        def tile(n, c):
            cols = pl.ds(pl.multiple_of(n * CHUNK, CHUNK), CHUNK)
            out = nn_dot(act[0], w_v[2, j, :, cols])
            p_out[mine, cols] = (by * out).astype(bf16)
            back = nt_dot(act[1], w_v[0, j, cols, :]) + nt_dot(act[2], w_v[1, j, cols, :])
            p_in[mine, cols] = back.astype(bf16)
            return c

        lax.fori_loop(0, width // CHUNK, tile, 0)
        return carry

    lax.fori_loop(0, local, finish, 0)

    for c in started:
        c.wait_send()
    acc = gb
    n1, n2, n3 = keys(row_of)
    down = lax.broadcasted_iota(jnp.int32, (gb.shape[0], row_of.shape[1]), 0)
    put_first, put_second = one_hot(n1 == down), one_hot(n2 == down)
    tail = jnp.zeros((gb.shape[0], CHUNK), f32)
    for q in range(width // CHUNK):
        cols = pl.ds(q * CHUNK, CHUNK)
        v = nn_dot(put_first, p_in[:, cols]) + nn_dot(put_second, p_out[:, cols])
        acc[:, cols] = v.astype(bf16)
        tail += nn_dot(one_hot(n3 + q == down), p_out[:, cols])
    acc[:, width:] = tail.astype(bf16)

    a1 = remote(acc.at[at_rows(diagonal * span, span)], r1.at[1], e_ss, e_rs, 0, {"expert": beside})
    a0 = remote(acc.at[at_rows(beside * span, span)], r1.at[0], e_ss, e_rs, 1, {"expert": beside})
    a1.start()
    a0.start()
    a1.wait_recv()
    s2[...] = (acc[at_rows(across * span, span), :].astype(f32) + r1[1].astype(f32)).astype(bf16)
    over = remote(s2.at[:, wide_cols[0]], r2, e_ss, e_rs, 2, {"expert": across})
    over.start()
    a0.wait_recv()
    s3[...] = (acc[at_rows(e * span, span), :].astype(f32) + r1[0].astype(f32)).astype(bf16)
    along, last = [], []
    for d in range(1, n_dp):
        to = lax.rem(z + d, n_dp)
        there = at_rows(to * PACK, PACK)
        for h, part in enumerate((s3, s2)):
            c = remote(
                part.at[there, wide_cols[1]], r3b.at[2 * d - 2 + h], e_ss, e_rs,
                1 + 2 * d + h, {"dp": to},
            )
            c.start()
            along.append(c)
    over.wait_recv()
    s4[...] = (s3[:, :FIRST].astype(f32) + r2[...].astype(f32)).astype(bf16)
    for d in range(1, n_dp):
        to = lax.rem(z + d, n_dp)
        c = remote(
            s4.at[at_rows(to * PACK, PACK)], r3.at[d - 1], e_ss, e_rs, 8 + d, {"dp": to}
        )
        c.start()
        last.append(c)
    here = at_rows(z * PACK, PACK)
    sums = [s3[here, FIRST:].astype(f32), s2[here, FIRST:].astype(f32)]
    for i, c in enumerate(along):
        c.wait_recv()
        sums[i % 2] += r3b[i].astype(f32)
    s5[...] = sums[1].astype(bf16)
    cross = remote(s5, r5, e_ss, e_rs, 12, {"expert": across})
    cross.start()
    final = s4[here, :].astype(f32)
    for d, c in enumerate(last):
        c.wait_recv()
        final += r3[d].astype(f32)
    cross.wait_recv()
    final = jnp.concatenate([final, sums[0] + r5[...].astype(f32)], axis=1)
    grad_ref[...] = final[:count, :width].astype(bf16)
    late = [
        jnp.concatenate([final[r * pieces + q : r * pieces + q + 1, width:] for q in range(pieces)], axis=1)
        for r in range(count - split)
    ]
    out_ref[...] = jnp.concatenate([final[count:, :width]] + late, axis=0).astype(bf16)

    for c in [a1, a0, over, cross] + along + last:
        c.wait_send()

    def sent(j, carry):
        for m in range(3):
            act_copy(j, m).wait_send()
        return carry

    lax.fori_loop(0, local, sent, 0)


def kernel_body(tokens, cotangent, routes, gate_probs, gate_proj, up_proj, down_proj):
    groups, n_dp = lax.axis_size("expert"), lax.axis_size("dp")
    blocks = groups * n_dp
    count, width = tokens.shape
    local, _, hidden_width = gate_proj.shape
    rows = blocks * CAP
    bf16, dma = jnp.bfloat16, pltpu.SemaphoreType.DMA
    full, span = width + CHUNK, n_dp * PACK
    return pl.pallas_call(
        glu_kernel,
        out_shape=[jax.ShapeDtypeStruct((count, width), bf16)] * 2,
        in_specs=[pl.BlockSpec(memory_space=pltpu.VMEM)] * 2
        + [pl.BlockSpec(memory_space=pltpu.SMEM)] * 2
        + [pl.BlockSpec(memory_space=pl.ANY)] * 3,
        out_specs=[pl.BlockSpec(memory_space=pltpu.VMEM)] * 2,
        scratch_shapes=[
            pltpu.VMEM((3, local, width, hidden_width), bf16),
            pltpu.VMEM((blocks * PACK, full), bf16),
            pltpu.VMEM((blocks, 8, 256), jnp.float32),
            pltpu.VMEM((local * rows, width), bf16),
            pltpu.VMEM((local * rows, width), bf16),
            pltpu.VMEM((local * rows, 128), jnp.float32),
            pltpu.VMEM((local, 3, rows, hidden_width), bf16),
            pltpu.VMEM((local, 3, rows, hidden_width), bf16),
            pltpu.VMEM((3, rows, hidden_width), bf16),
            pltpu.VMEM((256, width), bf16),
            pltpu.VMEM((256, width), bf16),
            pltpu.VMEM((2, span, full), bf16),
            pltpu.VMEM((span, full), bf16),
            pltpu.VMEM((span, FIRST), bf16),
            pltpu.VMEM((span, full), bf16),
            pltpu.VMEM((n_dp - 1, PACK, FIRST), bf16),
            pltpu.VMEM((2 * n_dp - 2, PACK, full - FIRST), bf16),
            pltpu.VMEM((span, FIRST), bf16),
            pltpu.VMEM((PACK, full - FIRST), bf16),
            pltpu.VMEM((PACK, full - FIRST), bf16),
            dma((3, local)),
            dma((21,)),
            dma((21,)),
            dma((local, 3)),
            dma((local, 3)),
            dma((13,)),
            dma((13,)),
        ],
        compiler_params=pltpu.CompilerParams(
            collective_id=0, has_side_effects=True, vmem_limit_bytes=VMEM_BYTES
        ),
    )(tokens, cotangent, routes, gate_probs, gate_proj, up_proj, down_proj)


def solution(mesh):
    in_specs = (
        P(("dp", "expert"), "tensor"),
        P(("dp", "expert"), "tensor"),
        P(("dp", "expert"), None),
        P(("dp", "expert"), None),
        P("expert", "tensor", "dp"),
        P("expert", "tensor", "dp"),
        P("expert", "dp", "tensor"),
    )
    out_specs = (P(("dp", "expert"), "tensor"), P(("dp", "expert"), "tensor"))
    small = (mesh.shape["dp"], mesh.shape["expert"], mesh.shape["tensor"]) == (4, 4, 2)
    return jax.shard_map(
        kernel_body if small else body,
        mesh=mesh, in_specs=in_specs, out_specs=out_specs, check_vma=False,
    )
```

```python
import jax
import jax.numpy as jnp
from jax import lax
from jax.experimental import pallas as pl
from jax.experimental.pallas import tpu as pltpu
from jax.sharding import PartitionSpec as P

EXPERTS = 16
CAP = 3
VMEM_BYTES = 67000000


def slot_tables(routes, gate_probs, num_experts, capacity):
    tok_count = routes.shape[0]
    top_count = routes.shape[1]
    flat_ids = routes.reshape(-1)
    pair_count = flat_ids.shape[0]
    same_expert = (flat_ids[:, None] == flat_ids[None, :]).astype(jnp.int32)
    earlier = (
        lax.broadcasted_iota(jnp.int32, (pair_count, pair_count), 1)
        < lax.broadcasted_iota(jnp.int32, (pair_count, pair_count), 0)
    ).astype(jnp.int32)
    slot_rank = jnp.sum(same_expert * earlier, axis=1)
    target = (flat_ids * capacity + slot_rank).reshape(tok_count, top_count)
    slot_ids = lax.broadcasted_iota(jnp.int32, (num_experts * capacity, tok_count, top_count), 0)
    matches = (slot_ids == target[None]).astype(jnp.float32)
    dispatch_tokens = jnp.sum(matches, axis=2)
    weighted_output_rows = jnp.sum(matches * gate_probs[None], axis=2)
    return (dispatch_tokens, weighted_output_rows)


def glu_terms(gate_activation_rows, up_activation_rows, backward_activation_rows):
    squashed = jax.nn.sigmoid(gate_activation_rows)
    swished = gate_activation_rows * squashed
    hidden = (swished * up_activation_rows).astype(jnp.bfloat16)
    grad_gate = (
        backward_activation_rows
        * up_activation_rows
        * squashed
        * (1.0 + gate_activation_rows * (1.0 - squashed))
    ).astype(jnp.bfloat16)
    grad_up = (backward_activation_rows * swished).astype(jnp.bfloat16)
    return (hidden, grad_gate, grad_up)


def body(tokens, cotangent, routes, gate_probs, gate_proj, up_proj, down_proj):
    quarter_slice = tokens.shape[1]
    local_experts = gate_proj.shape[0]
    groups = lax.axis_size("expert")
    dispatch_tokens, weighted_output_rows = slot_tables(routes, gate_probs, EXPERTS, CAP)
    sent_tokens = jnp.dot(
        dispatch_tokens.astype(jnp.bfloat16), tokens, preferred_element_type=jnp.float32
    ).astype(jnp.bfloat16)
    sent_grads = jnp.dot(
        weighted_output_rows, cotangent.astype(jnp.float32), precision=lax.Precision.HIGHEST
    ).astype(jnp.bfloat16)
    sent_tokens = sent_tokens.reshape(EXPERTS, CAP, quarter_slice)
    sent_grads = sent_grads.reshape(EXPERTS, CAP, quarter_slice)
    got_tokens, got_grads = (
        lax.all_to_all(sent_tokens, "expert", split_axis=0, concat_axis=0, tiled=True),
        lax.all_to_all(sent_grads, "expert", split_axis=0, concat_axis=0, tiled=True),
    )
    got_tokens = got_tokens.reshape(groups, local_experts, CAP, quarter_slice)
    got_grads = got_grads.reshape(groups, local_experts, CAP, quarter_slice)
    row_tokens, row_grads = (
        lax.all_gather(got_tokens, "dp", axis=0, tiled=True),
        lax.all_gather(got_grads, "dp", axis=0, tiled=True),
    )
    gate_part = jnp.einsum(
        "becd,edf->becf", row_tokens, gate_proj, preferred_element_type=jnp.float32
    )
    up_part = jnp.einsum("becd,edf->becf", row_tokens, up_proj, preferred_element_type=jnp.float32)
    back_part = jnp.einsum(
        "becd,efd->becf", row_grads, down_proj, preferred_element_type=jnp.float32
    )
    gate_activation_rows, up_activation_rows, backward_activation_rows = (
        lax.psum(gate_part.astype(jnp.bfloat16), "tensor").astype(jnp.float32),
        lax.psum(up_part.astype(jnp.bfloat16), "tensor").astype(jnp.float32),
        lax.psum(back_part.astype(jnp.bfloat16), "tensor").astype(jnp.float32),
    )
    hidden, grad_gate, grad_up = glu_terms(
        gate_activation_rows, up_activation_rows, backward_activation_rows
    )
    out_rows = lax.psum_scatter(
        jnp.einsum("becf,efd->becd", hidden, down_proj, preferred_element_type=jnp.float32).astype(
            jnp.bfloat16
        ),
        "dp",
        scatter_dimension=0,
        tiled=True,
    ).astype(jnp.float32)
    from_gate = jnp.einsum(
        "becf,edf->becd", grad_gate, gate_proj, preferred_element_type=jnp.float32
    )
    from_up = jnp.einsum("becf,edf->becd", grad_up, up_proj, preferred_element_type=jnp.float32)
    in_rows = lax.psum_scatter(
        (from_gate + from_up).astype(jnp.bfloat16), "dp", scatter_dimension=0, tiled=True
    ).astype(jnp.float32)
    out_rows = out_rows.astype(jnp.bfloat16)
    in_rows = in_rows.astype(jnp.bfloat16)
    back_out, back_in = (
        lax.all_to_all(out_rows, "expert", split_axis=0, concat_axis=0, tiled=True),
        lax.all_to_all(in_rows, "expert", split_axis=0, concat_axis=0, tiled=True),
    )
    flat_out = back_out.reshape(EXPERTS * CAP, quarter_slice).astype(jnp.float32)
    flat_in = back_in.reshape(EXPERTS * CAP, quarter_slice).astype(jnp.float32)
    mixture_layer_output = jnp.dot(
        weighted_output_rows.T, flat_out, precision=lax.Precision.HIGHEST
    ).astype(jnp.bfloat16)
    input_token_gradient = jnp.dot(
        dispatch_tokens.T, flat_in, precision=lax.Precision.HIGHEST
    ).astype(jnp.bfloat16)
    return (mixture_layer_output, input_token_gradient)


PACK = 16
CHUNK = 256
FIRST = 1024


def nt_dot(a, b):
    return lax.dot_general(a, b, (((1,), (1,)), ((), ())), preferred_element_type=jnp.float32)


def nn_dot(a, b):
    return jnp.dot(a, b, preferred_element_type=jnp.float32)


def glu_kernel(
    tok_ref, cot_ref, route_ref, prob_ref, wg_hbm, wu_hbm, wd_hbm, o_ref,
    w_v, gb, tab, xt, xg, pc, sbuf, rbuf, act, p_in, p_out, r1, s2, r2, s3, r3, r3b, s4, s5, r5,
    w_sem, g_ss, g_rs, x_ss, x_rs, e_ss, e_rs,
):
    f32, bf16 = jnp.float32, jnp.bfloat16
    count, width = tok_ref.shape
    split = PACK - count
    pieces = width // CHUNK
    local, hidden_width = wg_hbm.shape[0], wg_hbm.shape[2]
    rows = sbuf.shape[2]
    slots = local * rows
    n_dp = lax.axis_size("dp")
    z, e, t = lax.axis_index("dp"), lax.axis_index("expert"), lax.axis_index("tensor")
    across = lax.rem(e + 2, 4)
    beside = e + 1 - 2 * lax.rem(e, 2)
    diagonal = lax.rem(beside + 2, 4)
    other = 1 - t
    span = n_dp * PACK

    hbm = (wg_hbm, wu_hbm, wd_hbm)

    def weight(m, j):
        return pltpu.make_async_copy(hbm[m].at[j], w_v.at[m, j], w_sem.at[m, j])

    def remote(src, dst, ss, rs, i, where):
        return pltpu.make_async_remote_copy(
            src_ref=src, dst_ref=dst, send_sem=ss.at[i], recv_sem=rs.at[i],
            device_id=where, device_id_type=pl.DeviceIdType.MESH,
        )

    def at_rows(k, n):
        return pl.ds(pl.multiple_of(k, PACK), n)

    barrier = pltpu.get_barrier_semaphore()
    partners = [{"dp": lax.rem(z + d, n_dp)} for d in range(1, n_dp)]
    partners += [{"expert": across}, {"expert": beside}, {"tensor": other}]
    for p in partners:
        pl.semaphore_signal(barrier, inc=1, device_id=p, device_id_type=pl.DeviceIdType.MESH)
    for j in range(local):
        for m in range(3):
            weight(m, j).start()
    place = e * n_dp + z
    own = at_rows(place * PACK, PACK)
    tokens, cotangent = tok_ref[...].astype(f32), cot_ref[...].astype(f32)
    gb[own, :width] = jnp.concatenate([tokens, cotangent[:split]], axis=0).astype(bf16)
    tail = [
        cotangent[r : r + 1, q * CHUNK : (q + 1) * CHUNK]
        for r in range(split, count)
        for q in range(pieces)
    ]
    tail.append(jnp.zeros((PACK - len(tail), CHUNK), f32))
    gb[own, width:] = jnp.concatenate(tail, axis=0).astype(bf16)
    lane = lax.broadcasted_iota(jnp.int32, (8, 256), 1).astype(f32)
    group = lax.broadcasted_iota(jnp.int32, (8, 256), 0)
    expert = jnp.floor((lane + 0.5) / rows)
    within = lane - expert * rows
    block = jnp.floor((within + 0.5) / CAP)
    nth = (within - block * CAP).astype(jnp.int32)
    here = (block.astype(jnp.int32) == place) & (expert < local)
    expert = expert.astype(jnp.int32) + lax.rem(group, 4) * local
    seen = jnp.zeros((8, 256), jnp.int32)
    token = jnp.zeros((8, 256), f32)
    chance = jnp.zeros((8, 256), f32)
    for r in range(count):
        hits = jnp.zeros((8, 256), jnp.int32)
        for k in range(route_ref.shape[0]):
            hit = expert == route_ref[k, r]
            hits += hit.astype(jnp.int32)
            chance = jnp.where(hit & here & (seen == nth), prob_ref[k, r], chance)
        key = (place * PACK + 1 + r).astype(f32)
        token = jnp.where((hits > 0) & here & (seen == nth), key, token)
        seen += hits
    tab[pl.ds(place, 1)] = jnp.where(group < 4, token, chance)[None]
    p_in[slots:, :] = jnp.zeros((p_in.shape[0] - slots, width), bf16)
    p_out[slots:, :] = jnp.zeros((p_out.shape[0] - slots, width), bf16)
    pl.semaphore_wait(barrier, len(partners))

    wide_cols = (pl.ds(0, FIRST), pl.ds(FIRST, width + CHUNK - FIRST))

    def send(sent, src, to):
        i = len(started)
        c = remote(src, src, g_ss, g_rs, i, to)
        c.start()
        started.append(c)
        sent.append(c)

    def arrived(sent):
        for c in sent:
            c.wait_recv()

    def group_at(g, h):
        return gb.at[at_rows(g * span, span), wide_cols[h]]

    def table_at(g):
        return tab.at[pl.ds(g * n_dp, n_dp)]

    started, along, over = [], [], []
    one = tab.at[pl.ds(place, 1)]
    send(over, gb.at[own, wide_cols[1]], {"expert": across})
    for d in range(1, n_dp):
        to = {"dp": lax.rem(z + d, n_dp)}
        send(along, gb.at[own, wide_cols[0]], to)
        send(along, one, to)
    arrived(over)
    along_two, over_two, side = [], [], []
    facing = at_rows((across * n_dp + z) * PACK, PACK)
    for d in range(1, n_dp):
        to = {"dp": lax.rem(z + d, n_dp)}
        send(along_two, gb.at[own, wide_cols[1]], to)
        send(along_two, gb.at[facing, wide_cols[1]], to)
    arrived(along)
    send(over_two, group_at(e, 0), {"expert": across})
    send(over_two, table_at(e), {"expert": across})
    send(side, group_at(e, 0), {"expert": beside})
    send(side, table_at(e), {"expert": beside})
    arrived(along_two)
    send(side, group_at(e, 1), {"expert": beside})
    send(side, group_at(across, 1), {"expert": beside})
    arrived(over_two)
    send(side, group_at(across, 0), {"expert": beside})
    send(side, table_at(across), {"expert": beside})
    arrived(side)

    row_of = jnp.sum(tab[:, pl.ds(e, 1), :], axis=0)
    prob_of = jnp.sum(tab[:, pl.ds(e + 4, 1), :], axis=0)

    def keys(v):
        k = v - 1.0
        base = jnp.floor(k * (1.0 / PACK)) * PACK
        r = k - base
        second_key = jnp.where(r < split, k + count, -1.0)
        tail_key = jnp.where((r >= split) & (r < count), base + (r - split) * pieces, -1000.0)
        return k.astype(jnp.int32), second_key.astype(jnp.int32), tail_key.astype(jnp.int32)

    def one_hot(hit):
        return jnp.where(hit, 1.0, 0.0).astype(bf16)

    column = jnp.transpose(jnp.broadcast_to(row_of, (128, row_of.shape[1])))[:slots]
    pc[...] = jnp.transpose(jnp.broadcast_to(prob_of, (128, prob_of.shape[1])))[:slots]
    wide = jnp.concatenate([column, column], axis=1)
    k1, k2, k3 = keys(wide)
    lane = lax.broadcasted_iota(jnp.int32, (slots, 256), 1)
    pick_first, pick_second = one_hot(k1 == lane), one_hot(k2 == lane)
    scale = pc[:, 0:1]
    for q in range(width // CHUNK):
        cols = pl.ds(q * CHUNK, CHUNK)
        xt[:, cols] = nn_dot(pick_first, gb[:, cols]).astype(bf16)

    def act_copy(j, m):
        return pltpu.make_async_remote_copy(
            src_ref=sbuf.at[j, m], dst_ref=rbuf.at[j, m],
            send_sem=x_ss.at[j, m], recv_sem=x_rs.at[j, m],
            device_id={"tensor": other}, device_id_type=pl.DeviceIdType.MESH,
        )

    def project(j, carry, which=(0, 1, 2)):
        mine = pl.ds(j * rows, rows) if isinstance(j, int) else at_rows(j * rows, rows)
        for m in which:
            weight(m, j).wait()

            def tile(n, c):
                cols = pl.ds(pl.multiple_of(n * CHUNK, CHUNK), CHUNK)
                if m < 2:
                    part = nn_dot(xt[mine, :], w_v[m, j, :, cols])
                else:
                    part = nt_dot(xg[mine, :], w_v[m, j, cols, :])
                sbuf[j, m, :, cols] = part.astype(bf16)
                return c

            lax.fori_loop(0, hidden_width // CHUNK, tile, 0)
            act_copy(j, m).start()
        return carry

    project(0, 0, (0, 1))
    for q in range(width // CHUNK):
        cols = pl.ds(q * CHUNK, CHUNK)
        g = nn_dot(pick_second, gb[:, cols])
        g += nn_dot(one_hot(k3 + q == lane), gb[:, width:])
        xg[:, cols] = (scale * g).astype(bf16)
    project(0, 0, (2,))
    lax.fori_loop(1, local, project, 0)

    def finish(j, carry):
        mine = at_rows(j * rows, rows)
        for m in range(3):
            act_copy(j, m).wait_recv()

        def terms(n, c):
            cols = pl.ds(pl.multiple_of(n * CHUNK, CHUNK), CHUNK)
            total = [
                sbuf[j, m, :, cols].astype(f32) + rbuf[j, m, :, cols].astype(f32) for m in range(3)
            ]
            for m, v in enumerate(glu_terms(*total)):
                act[m, :, cols] = v
            return c

        lax.fori_loop(0, hidden_width // CHUNK, terms, 0)
        by = pc[mine, 0:1]

        def tile(n, c):
            cols = pl.ds(pl.multiple_of(n * CHUNK, CHUNK), CHUNK)
            out = nn_dot(act[0], w_v[2, j, :, cols])
            p_out[mine, cols] = (by * out).astype(bf16)
            back = nt_dot(act[1], w_v[0, j, cols, :]) + nt_dot(act[2], w_v[1, j, cols, :])
            p_in[mine, cols] = back.astype(bf16)
            return c

        lax.fori_loop(0, width // CHUNK, tile, 0)
        return carry

    lax.fori_loop(0, local, finish, 0)

    for c in started:
        c.wait_send()
    acc = gb
    n1, n2, n3 = keys(row_of)
    down = lax.broadcasted_iota(jnp.int32, (gb.shape[0], row_of.shape[1]), 0)
    put_first, put_second = one_hot(n1 == down), one_hot(n2 == down)
    tail = jnp.zeros((gb.shape[0], CHUNK), f32)
    for q in range(width // CHUNK):
        cols = pl.ds(q * CHUNK, CHUNK)
        v = nn_dot(put_first, p_in[:, cols]) + nn_dot(put_second, p_out[:, cols])
        acc[:, cols] = v.astype(bf16)
        tail += nn_dot(one_hot(n3 + q == down), p_out[:, cols])
    acc[:, width:] = tail.astype(bf16)

    a1 = remote(acc.at[at_rows(diagonal * span, span)], r1.at[1], e_ss, e_rs, 0, {"expert": beside})
    a0 = remote(acc.at[at_rows(beside * span, span)], r1.at[0], e_ss, e_rs, 1, {"expert": beside})
    a1.start()
    a0.start()
    a1.wait_recv()
    s2[...] = (acc[at_rows(across * span, span), :].astype(f32) + r1[1].astype(f32)).astype(bf16)
    over = remote(s2.at[:, wide_cols[0]], r2, e_ss, e_rs, 2, {"expert": across})
    over.start()
    a0.wait_recv()
    s3[...] = (acc[at_rows(e * span, span), :].astype(f32) + r1[0].astype(f32)).astype(bf16)
    along, last = [], []
    for d in range(1, n_dp):
        to = lax.rem(z + d, n_dp)
        there = at_rows(to * PACK, PACK)
        for h, part in enumerate((s3, s2)):
            c = remote(
                part.at[there, wide_cols[1]], r3b.at[2 * d - 2 + h], e_ss, e_rs,
                1 + 2 * d + h, {"dp": to},
            )
            c.start()
            along.append(c)
    over.wait_recv()
    s4[...] = (s3[:, :FIRST].astype(f32) + r2[...].astype(f32)).astype(bf16)
    for d in range(1, n_dp):
        to = lax.rem(z + d, n_dp)
        c = remote(
            s4.at[at_rows(to * PACK, PACK)], r3.at[d - 1], e_ss, e_rs, 8 + d, {"dp": to}
        )
        c.start()
        last.append(c)
    here = at_rows(z * PACK, PACK)
    sums = [s3[here, FIRST:].astype(f32), s2[here, FIRST:].astype(f32)]
    for i, c in enumerate(along):
        c.wait_recv()
        sums[i % 2] += r3b[i].astype(f32)
    s5[...] = sums[1].astype(bf16)
    cross = remote(s5, r5, e_ss, e_rs, 12, {"expert": across})
    cross.start()
    final = s4[here, :].astype(f32)
    for d, c in enumerate(last):
        c.wait_recv()
        final += r3[d].astype(f32)
    cross.wait_recv()
    final = jnp.concatenate([final, sums[0] + r5[...].astype(f32)], axis=1)
    unused = jnp.zeros((PACK - count, width), f32)
    o_ref[PACK:, :] = jnp.concatenate([final[:count, :width], unused], axis=0).astype(bf16)
    late = [
        jnp.concatenate([final[r * pieces + q : r * pieces + q + 1, width:] for q in range(pieces)], axis=1)
        for r in range(count - split)
    ]
    o_ref[:PACK, :] = jnp.concatenate([final[count:, :width]] + late + [unused], axis=0).astype(bf16)

    for c in [a1, a0, over, cross] + along + last:
        c.wait_send()

    def sent(j, carry):
        for m in range(3):
            act_copy(j, m).wait_send()
        return carry

    lax.fori_loop(0, local, sent, 0)


def kernel_body(tokens, cotangent, routes, gate_probs, gate_proj, up_proj, down_proj):
    groups, n_dp = lax.axis_size("expert"), lax.axis_size("dp")
    blocks = groups * n_dp
    count, width = tokens.shape
    local, _, hidden_width = gate_proj.shape
    rows = blocks * CAP
    bf16, dma = jnp.bfloat16, pltpu.SemaphoreType.DMA
    full, span = width + CHUNK, n_dp * PACK
    out = pl.pallas_call(
        glu_kernel,
        out_shape=jax.ShapeDtypeStruct((2 * PACK, width), bf16),
        in_specs=[pl.BlockSpec(memory_space=pltpu.VMEM)] * 2
        + [pl.BlockSpec(memory_space=pltpu.SMEM)] * 2
        + [pl.BlockSpec(memory_space=pl.ANY)] * 3,
        out_specs=pl.BlockSpec(memory_space=pltpu.VMEM),
        scratch_shapes=[
            pltpu.VMEM((3, local, width, hidden_width), bf16),
            pltpu.VMEM((blocks * PACK, full), bf16),
            pltpu.VMEM((blocks, 8, 256), jnp.float32),
            pltpu.VMEM((local * rows, width), bf16),
            pltpu.VMEM((local * rows, width), bf16),
            pltpu.VMEM((local * rows, 128), jnp.float32),
            pltpu.VMEM((local, 3, rows, hidden_width), bf16),
            pltpu.VMEM((local, 3, rows, hidden_width), bf16),
            pltpu.VMEM((3, rows, hidden_width), bf16),
            pltpu.VMEM((256, width), bf16),
            pltpu.VMEM((256, width), bf16),
            pltpu.VMEM((2, span, full), bf16),
            pltpu.VMEM((span, full), bf16),
            pltpu.VMEM((span, FIRST), bf16),
            pltpu.VMEM((span, full), bf16),
            pltpu.VMEM((n_dp - 1, PACK, FIRST), bf16),
            pltpu.VMEM((2 * n_dp - 2, PACK, full - FIRST), bf16),
            pltpu.VMEM((span, FIRST), bf16),
            pltpu.VMEM((PACK, full - FIRST), bf16),
            pltpu.VMEM((PACK, full - FIRST), bf16),
            dma((3, local)),
            dma((21,)),
            dma((21,)),
            dma((local, 3)),
            dma((local, 3)),
            dma((13,)),
            dma((13,)),
        ],
        compiler_params=pltpu.CompilerParams(
            collective_id=0, has_side_effects=True, vmem_limit_bytes=VMEM_BYTES
        ),
    )(tokens, cotangent, routes.T, gate_probs.T, gate_proj, up_proj, down_proj)
    return out[:count], out[PACK : PACK + count]


def solution(mesh):
    in_specs = (
        P(("dp", "expert"), "tensor"),
        P(("dp", "expert"), "tensor"),
        P(("dp", "expert"), None),
        P(("dp", "expert"), None),
        P("expert", "tensor", "dp"),
        P("expert", "tensor", "dp"),
        P("expert", "dp", "tensor"),
    )
    out_specs = (P(("dp", "expert"), "tensor"), P(("dp", "expert"), "tensor"))
    small = (mesh.shape["dp"], mesh.shape["expert"], mesh.shape["tensor"]) == (4, 4, 2)
    return jax.shard_map(
        kernel_body if small else body,
        mesh=mesh, in_specs=in_specs, out_specs=out_specs, check_vma=False,
    )
```
